512 devices in a mesh: wave: 128 (over y, z, core), lev: 4 (over x).
Axes of the slice: x: 4, y: 8, z: 8, core: 2. Of those that a mesh axis runs over, the one named last changes fastest.
Arguments:
- spectral: bfloat16 [1280, 12, 2, 1280], P('wave', 'lev'), may hold values from -6 to 6
- legendre: bfloat16 [1280, 128, 1280], P('wave'), may hold values from -0.0048828125 to 0.0048828125
- wave_order: int32 [1280], replicated, may hold values from 0 to 1279, each once
- nlon: int32 [128], replicated, may hold values from 20 to 5136, as said below
Outputs:
- grid: float32 [12, 256, 5136], P(None, 'wave', 'lev')
The draws below stay inside these ranges and needn't reach their ends.
Inputs may be any that keep to these rules, and one draw needn't show every extreme that they name: `wave_order`: each wavenumber 0 to 1279 stands at exactly one position. `nlon`: ascending and distinct, each 20 + 4 r for a whole r of 0 to 1279; the last is 5136.
All inputs are finite; a program needn't handle non-finite values.
Results may differ from the reference program's by a relative error of at most 0.0037.
Values may be sent and summed in bfloat16 or wider, within the bound.
A program may use at most 192 MiB of HBM per device.

```python
import math
import jax
import jax.numpy as jnp
from jax import lax

WAVES = 1280
NLON_MAX = 5136
FL = 12
HLAT = 128


def draw_nlon(key, part):
    key = jax.random.fold_in(key, 7)
    order = jax.random.permutation(key, WAVES - 1).astype(jnp.int32)
    picked = jnp.sort(order[:HLAT - 1])
    picked = jnp.concatenate([picked, jnp.full((1,), WAVES - 1, jnp.int32)])
    return (20 + 4 * picked).astype(jnp.int32)


def level_of(own_key, shape, pieces, smallest, high):
    def one(position, parts):
        heights = jax.random.uniform(jax.random.fold_in(jax.random.fold_in(own_key, 6), position), (parts,), jnp.float32, smallest / len(pieces), high / len(pieces))
        return jnp.repeat(jnp.exp(heights), shape[position] // parts).reshape((-1,) + (1,) * (len(shape) - position - 1))

    level = one(*pieces[0])
    for cut in pieces[1:]:
        level = level * one(*cut)
    return level


def scatter_about(stream_key, extent, scale, bound, split=(), kind=jnp.bfloat16):
    entries = jax.random.normal(stream_key, extent, jnp.float32) * scale
    if len(split) > 0:
        entries = level_of(stream_key, extent, split, -0.22, 0.18) * entries
    return jnp.clip(entries, min=-bound, max=bound).astype(kind)


def setup_inputs(seed: int = 0) -> dict:
    arg_keys = jax.random.split(jax.random.key(seed), 5)
    spectral = scatter_about(arg_keys[0], (WAVES, FL, 2, WAVES), 1.0, 6.0, ((0, 128), (1, 4)))
    legendre = scatter_about(arg_keys[1], (WAVES, HLAT, WAVES), (WAVES * WAVES) ** -0.5, 0.0048828125, ((0, 128),))
    wave_order = jax.random.permutation(arg_keys[2], WAVES).astype(jnp.int32)
    nlon = draw_nlon(jax.random.fold_in(arg_keys[4], 71), 0)
    return dict(spectral=spectral, legendre=legendre, wave_order=wave_order, nlon=nlon)


def fourier_table(wave_order, count, first, width):
    columns = first + jnp.arange(width, dtype=jnp.int32)
    phase = (wave_order[:, None] * columns[None, :]) % count
    angle = phase.astype(jnp.float32) * (2.0 * math.pi) / count.astype(jnp.float32)
    keep = (2 * wave_order[:, None] < count) & (columns[None, :] < count)
    weight = jnp.where(wave_order == 0, 1.0, 2.0).astype(jnp.float32)[:, None]
    cosine = jnp.where(keep, weight * jnp.cos(angle), 0.0)
    sine = jnp.where(keep, -weight * jnp.sin(angle), 0.0)
    return jnp.concatenate([cosine, sine], 0).astype(jnp.bfloat16)


def synthesize(coeffs, wave_order, count, first, width):
    mixed = jnp.concatenate([coeffs[:, :, 0], coeffs[:, :, 1]], 0).astype(jnp.float32)
    table = fourier_table(wave_order, count, first, width).astype(jnp.float32)
    return lax.dot_general(mixed, table, (((0,), (0,)), ((), ())), precision=lax.Precision.HIGHEST, preferred_element_type=jnp.float32)


def reference(spectral, legendre, wave_order, nlon):
    offsets = jnp.arange(WAVES, dtype=jnp.int32)
    parity = jnp.where(offsets % 2 == 0, 1.0, -1.0).astype(jnp.bfloat16)

    def one_wave(item):
        coeffs, table, wave = item
        live = offsets < WAVES - wave
        flat = jnp.where(live[None, None, :], coeffs, jnp.zeros((), jnp.bfloat16)).reshape(FL * 2, WAVES)
        north = jnp.dot(table, flat.T, preferred_element_type=jnp.float32)
        south = jnp.dot(table * parity[None, :], flat.T, preferred_element_type=jnp.float32)
        paired = jnp.stack([north.astype(jnp.bfloat16), south.astype(jnp.bfloat16)[::-1]], 1)
        return paired.reshape(2 * HLAT, FL, 2)

    fourier = lax.map(one_wave, (spectral, legendre, wave_order))
    lat_index = jnp.arange(2 * HLAT, dtype=jnp.int32)
    row_index = jnp.where(lat_index % 2 == 0, lat_index // 2, HLAT - 1 - lat_index // 2)
    counts = nlon[row_index]

    def one_lat(item):
        coeffs, count = item
        return synthesize(coeffs, wave_order, count, 0, NLON_MAX)

    grid = lax.map(one_lat, (jnp.transpose(fourier, (1, 0, 2, 3)), counts))
    return jnp.transpose(grid, (1, 0, 2))
```

```python
import functools
import math

import jax
import jax.numpy as jnp
from jax import lax
from jax.experimental import pallas as pl
from jax.experimental.pallas import tpu as pltpu
from jax.sharding import PartitionSpec as P

MESH = pl.DeviceIdType.MESH
F32 = jnp.float32
BF16 = jnp.bfloat16
LANES = 128
HALF = LANES // 2
SPAN = 256
STEP = 16
NT = (((1,), (1,)), ((), ()))


def iota(shape, dim):
    return lax.broadcasted_iota(jnp.int32, shape, dim)


def sincos(x, n, inv, far):
    if far:
        x = x - jnp.floor(x * inv + 0.5) * n
    x = 4.0 * x
    k = jnp.floor(x * inv + 0.5)
    a = (x - k * n) * (inv * (math.pi / 2))
    q = k.astype(jnp.int32)
    z = a * a
    s = a + a * z * (-1.6666654611e-1 + z * (8.3321608736e-3 + z * -1.9515295891e-4))
    c = 1.0 - 0.5 * z + z * z * (
        4.166664568298827e-2 + z * (-1.388731625493765e-3 + z * 2.443315711809948e-5)
    )
    odd = (q & 1) == 1
    cos, sin = jnp.where(odd, s, c), jnp.where(odd, c, s)
    cos = jnp.where(((q + 1) & 2) == 2, -cos, cos)
    sin = jnp.where((q & 2) == 2, -sin, sin)
    return cos, sin


def kernel(
    chips, cores, levs, quarter,
    spec_ref, leg_ref, order_s, nlon_s, order_v, out_ref,
    lbuf, xbuf, zbuf, send1, recv1, send2, recv2, table, twist, mixed, gbuf, vbuf,
    leg_sem, s1_sem, r1_sem, s2_sem, r2_sem,
):
    slots, half, width = leg_ref.shape
    fields = spec_ref.shape[1]
    total = fields * levs
    w = lax.axis_index("wave")
    x = lax.axis_index("lev")
    chip, core = w // cores, lax.rem(w, cores)

    def leg_copy(p):
        return pltpu.make_async_copy(leg_ref.at[p], lbuf.at[p], leg_sem.at[p])

    for p in range(slots):
        leg_copy(p).start()

    barrier = pltpu.get_barrier_semaphore()

    def near(d):
        return lax.rem(core + d // levs, cores), lax.rem(x + d % levs, levs)

    def greet(d, carry):
        there = lax.rem(chip + d, chips) * cores + core
        pl.semaphore_signal(barrier, inc=1, device_id=(there, x), device_id_type=MESH)
        return carry

    lax.fori_loop(1, chips, greet, 0)
    group = cores * levs
    for d in range(1, group):
        c2, x2 = near(d)
        pl.semaphore_signal(barrier, inc=1, device_id=(chip * cores + c2, x2), device_id_type=MESH)

    rows_v = order_v.shape[0]
    lane = iota((1, half), 1)
    device = lax.rem(lane, chips) * cores + lane // chips
    high, low = (order_v[...] // 256).astype(F32).astype(BF16), lax.rem(order_v[...], 256).astype(F32).astype(BF16)
    for p in range(slots):
        place = device * slots + p
        pick = (iota((order_v.shape[1], half), 0) == lax.rem(place, order_v.shape[1])).astype(F32).astype(BF16)
        both = 256.0 * jnp.dot(high, pick, preferred_element_type=F32) + jnp.dot(low, pick, preferred_element_type=F32)
        row = iota((rows_v, half), 0) == place // order_v.shape[1]
        vbuf[p : p + 1] = jnp.sum(jnp.where(row, both, 0.0), 0, keepdims=True)

    offset = iota((1, width), 1)
    parity = (1 - 2 * lax.rem(offset, 2)).astype(F32)
    zbuf[...] = jnp.zeros_like(zbuf)
    for p in range(slots):
        live = offset < width - order_s[w * slots + p]
        for f in range(fields):
            coeffs = jnp.where(live, spec_ref[p, f].astype(F32), 0.0)
            xbuf[p, 2 * f : 2 * f + 2] = coeffs
            xbuf[p, 8 + 2 * f : 8 + 2 * f + 2] = coeffs * parity
        leg_copy(p).wait()
        sums = lax.dot_general(xbuf[p].astype(BF16), lbuf[p], NT, preferred_element_type=F32)
        n = 2 * fields
        zbuf[n * p : n * p + n] = sums[0:n]
        zbuf[HALF + n * p : HALF + n * p + n] = sums[8 : 8 + n]

    z = zbuf[...].astype(BF16).astype(F32)
    north = iota((LANES, half), 0) < HALF
    pair = jnp.concatenate([jnp.where(north, z, 0.0), jnp.where(north, 0.0, z)], 1).astype(BF16)
    h, g = iota((half, 2 * half), 0), iota((half, 2 * half), 1)
    route = ((g == h) | ((g == 2 * half - 1 - h) & (g >= half))).astype(F32).astype(BF16)
    rows = lax.dot_general(route, pair, NT, preferred_element_type=F32)
    send1[...] = rows.reshape(chips, cores, LANES)

    pl.semaphore_wait(barrier, chips - 1 + group - 1)

    def first_copy(src, dst, there):
        return pltpu.make_async_remote_copy(
            src_ref=src, dst_ref=dst, send_sem=s1_sem, recv_sem=r1_sem,
            device_id=(there, x), device_id_type=MESH,
        )

    def push(d, carry):
        to = lax.rem(chip + d, chips)
        first_copy(send1.at[to], recv1.at[chip], to * cores + core).start()
        return carry

    lax.fori_loop(1, chips, push, 0)
    recv1[pl.ds(chip, 1)] = send1[pl.ds(chip, 1)]

    counts = [nlon_s[w].astype(F32), nlon_s[half - 1 - w].astype(F32)]
    inverse = [1.0 / jnp.full((1, half), n, F32) for n in counts]
    fine = iota((STEP, half), 0).astype(F32)
    for ns in range(2):
        n, inv = counts[ns], inverse[ns]
        for p in range(slots):
            m = vbuf[p : p + 1]
            cb, sb = sincos(m * fine, n, inv, False)
            ca, sa = sincos(m * (STEP * fine), n, inv, False)
            for a in range(SPAN // STEP):
                c1, s1 = ca[a : a + 1], sa[a : a + 1]
                here = pl.ds(a * STEP, STEP)
                table[ns, here, p * half : (p + 1) * half] = (c1 * cb - s1 * sb).astype(BF16)
                table[ns, here, (slots + p) * half : (slots + p + 1) * half] = (-(c1 * sb) - s1 * cb).astype(BF16)

    everything = first_copy(send1.at[pl.ds(0, chips - 1)], recv1.at[pl.ds(0, chips - 1)], lax.rem(chip + 1, chips) * cores + core)
    everything.wait_recv()
    got = recv1[...]
    for c in range(cores):
        send2[c] = got[:, c, :].astype(BF16)

    second = []
    for d in range(1, group):
        c2, x2 = near(d)
        second.append(
            pltpu.make_async_remote_copy(
                src_ref=send2.at[c2], dst_ref=recv2.at[x, core], send_sem=s2_sem.at[d], recv_sem=r2_sem.at[d],
                device_id=(chip * cores + c2, x2), device_id_type=MESH,
            )
        )
    for copy in second:
        copy.start()
    recv2[x, core] = send2[core]

    first = x * quarter
    spans = pl.cdiv(quarter, SPAN)
    starts = (first + SPAN * iota((8, half), 0)).astype(F32)
    for ns in range(2):
        n, inv = counts[ns], inverse[ns]
        for p in range(slots):
            m = vbuf[p : p + 1]
            weight = jnp.where(2.0 * m < n, jnp.where(m == 0.0, 1.0, 2.0), 0.0)
            ct, st = sincos(m * starts, n, inv, True)
            twist[ns, p, 0] = ct * weight
            twist[ns, p, 1] = st * weight

    f16 = iota((STEP, LANES), 0)
    gap = iota((STEP, LANES), 1) - 2 * f16
    parts = [(f16 >= fields * v) & (f16 < fields * (v + 1)) for v in range(levs)]
    picks = []
    for ns in range(2):
        for c in range(2):
            for p in range(slots):
                at = HALF * ns + 2 * fields * p + c
                picks.append(
                    jnp.concatenate(
                        [((gap == at - 2 * fields * v) & parts[v]).astype(F32) for v in range(levs)], 1
                    ).astype(BF16)
                )
    choice = jnp.concatenate(picks, 0)

    for copy in second:
        copy.wait_recv()
    arrived = jnp.concatenate([recv2[v].reshape(half, LANES) for v in range(levs)], 1)
    mixed[...] = lax.dot_general(choice, arrived, NT, preferred_element_type=F32)

    for ns in range(2):
        for p in range(slots):
            at = STEP * (2 * slots * ns + p)
            re, im = mixed[at : at + STEP], mixed[at + STEP * slots : at + STEP * slots + STEP]
            for s in range(spans):
                ct, st = twist[ns, p, 0, s : s + 1], twist[ns, p, 1, s : s + 1]
                here = pl.ds(s * STEP, STEP)
                gbuf[ns, here, p * half : (p + 1) * half] = (re * ct - im * st).astype(BF16)
                gbuf[ns, here, (slots + p) * half : (slots + p + 1) * half] = (re * st + im * ct).astype(BF16)
        grid = lax.dot_general(gbuf[ns], table[ns], NT, preferred_element_type=F32)
        for s in range(spans):
            size = min(SPAN, quarter - s * SPAN)
            column = first + s * SPAN + iota((total, size), 1)
            keep = column < nlon_s[w if ns == 0 else half - 1 - w]
            out_ref[ns, :, s * SPAN : s * SPAN + size] = jnp.where(
                keep, grid[s * STEP : s * STEP + total, :size], 0.0
            )
    everything.wait_send()
    for copy in second:
        copy.wait_send()


def shards(spectral, legendre, wave_order, nlon):
    slots, half, width = legendre.shape
    fields = spectral.shape[1]
    waves, levs = lax.axis_size("wave"), lax.axis_size("lev")
    cores = 2
    chips = waves // cores
    quarter = (4 * width + 16) // levs
    spans = pl.cdiv(quarter, SPAN)
    vmem = pl.BlockSpec(memory_space=pltpu.VMEM)
    smem = pl.BlockSpec(memory_space=pltpu.SMEM)
    dma = pltpu.SemaphoreType.DMA
    order_rows = wave_order.reshape(-1, min(LANES, wave_order.shape[0] // slots))
    grid = pl.pallas_call(
        functools.partial(kernel, chips, cores, levs, quarter),
        out_shape=jax.ShapeDtypeStruct((2, fields * levs, quarter), F32),
        in_specs=[vmem, pl.BlockSpec(memory_space=pl.ANY), smem, smem, vmem],
        out_specs=vmem,
        scratch_shapes=[
            pltpu.VMEM((slots, half, width), BF16),
            pltpu.VMEM((slots, 16, width), F32),
            pltpu.VMEM((LANES, half), F32),
            pltpu.VMEM((chips, cores, LANES), F32),
            pltpu.VMEM((chips, cores, LANES), F32),
            pltpu.VMEM((cores, chips, LANES), BF16),
            pltpu.VMEM((levs, cores, chips, LANES), BF16),
            pltpu.VMEM((2, SPAN, 2 * slots * half), BF16),
            pltpu.VMEM((2, slots, 2, 8, half), F32),
            pltpu.VMEM((4 * slots * STEP, half), F32),
            pltpu.VMEM((2, spans * STEP, 2 * slots * half), BF16),
            pltpu.VMEM((16, half), F32),
            dma((slots,)),
            dma,
            dma,
            dma((cores * levs,)),
            dma((cores * levs,)),
        ],
        compiler_params=pltpu.CompilerParams(
            collective_id=0, has_side_effects=True, vmem_limit_bytes=40 * 1024 * 1024
        ),
    )(spectral, legendre, wave_order, nlon, order_rows)
    return jnp.transpose(grid, (1, 0, 2))


def solution(mesh):
    placed = (P("wave", "lev", None, None), P("wave", None, None), P(), P())
    return jax.shard_map(
        shards, mesh=mesh, in_specs=placed, out_specs=P(None, "wave", "lev"), check_vma=False
    )
```

```python
import functools
import math

import jax
import jax.numpy as jnp
from jax import lax
from jax.experimental import pallas as pl
from jax.experimental.pallas import tpu as pltpu
from jax.sharding import PartitionSpec as P

MESH = pl.DeviceIdType.MESH
F32 = jnp.float32
BF16 = jnp.bfloat16
LANES = 128
HALF = LANES // 2
SPAN = 256
STEP = 16
NT = (((1,), (1,)), ((), ()))


def iota(shape, dim):
    return lax.broadcasted_iota(jnp.int32, shape, dim)


def sincos(x, n, inv, far):
    if far:
        x = x - jnp.floor(x * inv + 0.5) * n
    x = 4.0 * x
    k = jnp.floor(x * inv + 0.5)
    a = (x - k * n) * (inv * (math.pi / 2))
    q = k.astype(jnp.int32)
    z = a * a
    s = a + a * z * (-1.6666654611e-1 + z * (8.3321608736e-3 + z * -1.9515295891e-4))
    c = 1.0 - 0.5 * z + z * z * (
        4.166664568298827e-2 + z * (-1.388731625493765e-3 + z * 2.443315711809948e-5)
    )
    odd = (q & 1) == 1
    cos, sin = jnp.where(odd, s, c), jnp.where(odd, c, s)
    cos = jnp.where(((q + 1) & 2) == 2, -cos, cos)
    sin = jnp.where((q & 2) == 2, -sin, sin)
    return cos, sin


def kernel(
    chips, cores, levs, quarter,
    spec_hbm, leg_ref, order_hbm, nlon_hbm, rows_hbm, out_ref,
    spec_ref, order_s, nlon_s, order_v, lbuf, xbuf, zbuf, send1, recv1, send2, recv2, table, twist, mixed, gbuf, vbuf,
    in_sem, leg_sem, s1_sem, r1_sem, s2_sem, r2_sem,
):
    slots, half, width = leg_ref.shape
    fields = spec_ref.shape[1]
    total = fields * levs
    w = lax.axis_index("wave")
    x = lax.axis_index("lev")
    chip, core = w // cores, lax.rem(w, cores)

    inputs = [
        pltpu.make_async_copy(src, dst, in_sem.at[i])
        for i, (src, dst) in enumerate(
            [(spec_hbm, spec_ref), (order_hbm, order_s), (nlon_hbm, nlon_s), (rows_hbm, order_v)]
        )
    ]
    legs = [pltpu.make_async_copy(leg_ref.at[p], lbuf.at[p], leg_sem.at[p]) for p in range(slots)]

    side = math.isqrt(chips)
    y, z = chip // side, lax.rem(chip, side)
    ys = [lax.rem(y + d, side) for d in range(side)]
    zs = [lax.rem(z + d, side) for d in range(side)]
    cs = [lax.rem(core + d, cores) for d in range(cores)]
    xs = [lax.rem(x + d, levs) for d in range(levs)]

    def hops(d, n):
        return min(d, n - d)

    def far_first(n1, n2, weight):
        pairs = [(d, e) for d in range(n1) for e in range(n2) if d or e]
        return sorted(pairs, key=lambda d: -hops(d[0], n1) - weight * hops(d[1], n2))

    mates = [(ys[d], cs[e]) for d, e in far_first(side, cores, 0.1)]
    rest = [(zs[d], xs[e]) for d, e in far_first(side, levs, 1)]

    def mate_id(there):
        return ((there[0] * side + z) * cores + there[1], x)

    def rest_id(there):
        return ((y * side + there[0]) * cores + core, there[1])

    barrier = pltpu.get_barrier_semaphore()
    for i, there in enumerate([rest_id(r) for r in rest] + [mate_id(r) for r in mates]):
        if i == side:
            for copy in inputs + legs:
                copy.start()
        pl.semaphore_signal(barrier, inc=1, device_id=there, device_id_type=MESH)
    for copy in inputs:
        copy.wait()

    offset = iota((1, width), 1)
    parity = (1 - 2 * lax.rem(offset, 2)).astype(F32)
    zbuf[...] = jnp.zeros_like(zbuf)
    n = 2 * fields
    for p in range(slots):
        live = offset < width - order_s[w * slots + p]
        for f in range(fields):
            coeffs = jnp.where(live, spec_ref[p, f].astype(F32), 0.0)
            xbuf[p, 2 * f : 2 * f + 2] = coeffs
            xbuf[p, 8 + 2 * f : 8 + 2 * f + 2] = coeffs * parity
    for p in range(slots):
        legs[p].wait()
        sums = lax.dot_general(xbuf[p].astype(BF16), lbuf[p], NT, preferred_element_type=F32)
        zbuf[n * p : n * p + n] = sums[0:n]
        zbuf[HALF + n * p : HALF + n * p + n] = sums[8 : 8 + n]

    total_mates = side * cores
    values = zbuf[...].astype(BF16).astype(F32)
    north = iota((LANES, half), 0) < HALF
    pair = jnp.concatenate([jnp.where(north, values, 0.0), jnp.where(north, 0.0, values)], 1).astype(BF16)
    r, g = iota((half, 2 * half), 0), iota((half, 2 * half), 1)
    h = (r // total_mates * side + lax.rem(r, side)) * cores + lax.rem(r // side, cores)
    route = ((g == h) | ((g == 2 * half - 1 - h) & (g >= half))).astype(F32).astype(BF16)
    send1[...] = lax.dot_general(route, pair, NT, preferred_element_type=F32)

    pl.semaphore_wait(barrier, len(mates) + len(rest))

    def block(i):
        return pl.ds(pl.multiple_of(i * side, side), side)

    def remote(src, dst, sems, there):
        return pltpu.make_async_remote_copy(
            src_ref=src, dst_ref=dst, send_sem=sems[0], recv_sem=sems[1], device_id=there, device_id_type=MESH
        )

    own = y * cores + core
    for there in mates:
        remote(send1.at[block(there[0] * cores + there[1])], recv1.at[block(own)], (s1_sem, r1_sem), mate_id(there)).start()
    recv1[block(own)] = send1[block(own)]

    rows_v = order_v.shape[0]
    lane = iota((1, half), 1)
    device = (lax.rem(lane, total_mates) // cores * side + lane // total_mates) * cores + lax.rem(lane, cores)
    high, low = (order_v[...] // 256).astype(F32).astype(BF16), lax.rem(order_v[...], 256).astype(F32).astype(BF16)
    for p in range(slots):
        place = device * slots + p
        pick = (iota((order_v.shape[1], half), 0) == lax.rem(place, order_v.shape[1])).astype(F32).astype(BF16)
        both = 256.0 * jnp.dot(high, pick, preferred_element_type=F32) + jnp.dot(low, pick, preferred_element_type=F32)
        row = iota((rows_v, half), 0) == place // order_v.shape[1]
        vbuf[p : p + 1] = jnp.sum(jnp.where(row, both, 0.0), 0, keepdims=True)

    counts = [nlon_s[w].astype(F32), nlon_s[half - 1 - w].astype(F32)]
    inverse = [1.0 / jnp.full((1, half), n, F32) for n in counts]
    fine = iota((STEP, half), 0).astype(F32)
    for ns in range(2):
        n, inv = counts[ns], inverse[ns]
        for p in range(slots):
            m = vbuf[p : p + 1]
            cb, sb = sincos(m * fine, n, inv, False)
            ca, sa = sincos(m * (STEP * fine), n, inv, False)
            for a in range(SPAN // STEP):
                c1, s1 = ca[a : a + 1], sa[a : a + 1]
                here = pl.ds(a * STEP, STEP)
                table[ns, here, p * half : (p + 1) * half] = (c1 * cb - s1 * sb).astype(BF16)
                table[ns, here, (slots + p) * half : (slots + p + 1) * half] = (-(c1 * sb) - s1 * cb).astype(BF16)

    most = pl.ds(0, side * (total_mates - 1))
    first_all = remote(send1.at[most], recv1.at[most], (s1_sem, r1_sem), mate_id(mates[0]))
    first_all.wait_recv()
    for i in range(side):
        send2[i] = recv1[pl.ds(i, total_mates, stride=side)].astype(BF16)
    for there in rest:
        remote(send2.at[there[0]], recv2.at[x * side + z], (s2_sem, r2_sem), rest_id(there)).start()
    recv2[x * side + z] = send2[z]

    first = x * quarter
    spans = pl.cdiv(quarter, SPAN)
    starts = (first + SPAN * iota((8, half), 0)).astype(F32)
    for ns in range(2):
        n, inv = counts[ns], inverse[ns]
        for p in range(slots):
            m = vbuf[p : p + 1]
            weight = jnp.where(2.0 * m < n, jnp.where(m == 0.0, 1.0, 2.0), 0.0)
            ct, st = sincos(m * starts, n, inv, True)
            twist[ns, p, 0] = ct * weight
            twist[ns, p, 1] = st * weight

    f16 = iota((STEP, LANES), 0)
    gap = iota((STEP, LANES), 1) - 2 * f16
    parts = [(f16 >= fields * v) & (f16 < fields * (v + 1)) for v in range(levs)]
    picks = []
    for ns in range(2):
        for c in range(2):
            for p in range(slots):
                at = HALF * ns + 2 * fields * p + c
                picks.append(
                    jnp.concatenate(
                        [((gap == at - 2 * fields * v) & parts[v]).astype(F32) for v in range(levs)], 1
                    ).astype(BF16)
                )
    choice = jnp.concatenate(picks, 0)

    most = pl.ds(0, side * levs - 1)
    second_all = remote(recv2.at[most], recv2.at[most], (s2_sem, r2_sem), rest_id(rest[0]))
    second_all.wait_recv()
    arrived = jnp.concatenate(
        [recv2[v * side : (v + 1) * side].reshape(half, LANES) for v in range(levs)], 1
    )
    mixed[...] = lax.dot_general(choice, arrived, NT, preferred_element_type=F32)

    for ns in range(2):
        for p in range(slots):
            at = STEP * (2 * slots * ns + p)
            re, im = mixed[at : at + STEP], mixed[at + STEP * slots : at + STEP * slots + STEP]
            for s in range(spans):
                ct, st = twist[ns, p, 0, s : s + 1], twist[ns, p, 1, s : s + 1]
                here = pl.ds(s * STEP, STEP)
                gbuf[ns, here, p * half : (p + 1) * half] = (re * ct - im * st).astype(BF16)
                gbuf[ns, here, (slots + p) * half : (slots + p + 1) * half] = (re * st + im * ct).astype(BF16)
        grid = lax.dot_general(gbuf[ns], table[ns], NT, preferred_element_type=F32)
        for s in range(spans):
            size = min(SPAN, quarter - s * SPAN)
            place = first + s * SPAN + iota((total, size), 1)
            keep = place < nlon_s[w if ns == 0 else half - 1 - w]
            out_ref[ns * total : (ns + 1) * total, s * SPAN : s * SPAN + size] = jnp.where(
                keep, grid[s * STEP : s * STEP + total, :size], 0.0
            )
    first_all.wait_send()
    second_all.wait_send()


def shards(spectral, legendre, wave_order, nlon):
    slots, half, width = legendre.shape
    fields = spectral.shape[1]
    waves, levs = lax.axis_size("wave"), lax.axis_size("lev")
    cores = 2
    chips = waves // cores
    side = math.isqrt(chips)
    quarter = (4 * width + 16) // levs
    spans = pl.cdiv(quarter, SPAN)
    hbm = pl.BlockSpec(memory_space=pltpu.HBM)
    dma = pltpu.SemaphoreType.DMA
    order_rows = wave_order.reshape(-1, min(LANES, wave_order.shape[0] // slots))
    grid = pl.pallas_call(
        functools.partial(kernel, chips, cores, levs, quarter),
        out_shape=pltpu.VMEM((2 * fields * levs, quarter), F32),
        in_specs=[hbm] * 5,
        out_specs=pl.BlockSpec(memory_space=pltpu.VMEM),
        scratch_shapes=[
            pltpu.VMEM(spectral.shape, BF16),
            pltpu.SMEM(wave_order.shape, jnp.int32),
            pltpu.SMEM(nlon.shape, jnp.int32),
            pltpu.VMEM(order_rows.shape, jnp.int32),
            pltpu.VMEM((slots, half, width), BF16),
            pltpu.VMEM((slots, 16, width), F32),
            pltpu.VMEM((LANES, half), F32),
            pltpu.VMEM((half, LANES), F32),
            pltpu.VMEM((half, LANES), F32),
            pltpu.VMEM((side, side * cores, LANES), BF16),
            pltpu.VMEM((levs * side, side * cores, LANES), BF16),
            pltpu.VMEM((2, SPAN, 2 * slots * half), BF16),
            pltpu.VMEM((2, slots, 2, 8, half), F32),
            pltpu.VMEM((4 * slots * STEP, half), F32),
            pltpu.VMEM((2, spans * STEP, 2 * slots * half), BF16),
            pltpu.VMEM((16, half), F32),
            dma((4,)),
            dma((slots,)),
            dma,
            dma,
            dma,
            dma,
        ],
        compiler_params=pltpu.CompilerParams(
            collective_id=0, has_side_effects=True, vmem_limit_bytes=64 * 1024 * 1024 - 400000
        ),
    )(spectral, legendre, wave_order, nlon, order_rows)
    return jnp.transpose(grid.reshape(2, fields * levs, quarter), (1, 0, 2))


def solution(mesh):
    placed = (P("wave", "lev", None, None), P("wave", None, None), P(), P())
    return jax.shard_map(
        shards, mesh=mesh, in_specs=placed, out_specs=P(None, "wave", "lev"), check_vma=False
    )
```

```python
import functools
import math

import jax
import jax.numpy as jnp
from jax import lax
from jax.experimental import pallas as pl
from jax.experimental.pallas import tpu as pltpu
from jax.sharding import PartitionSpec as P

MESH = pl.DeviceIdType.MESH
F32 = jnp.float32
BF16 = jnp.bfloat16
LANES = 128
HALF = LANES // 2
SPAN = 256
GROUPS = 2
STEP = 16
NT = (((1,), (1,)), ((), ()))


def iota(shape, dim):
    return lax.broadcasted_iota(jnp.int32, shape, dim)


def sincos(x, n, inv, far):
    if far:
        x = x - jnp.floor(x * inv + 0.5) * n
    x = 4.0 * x
    k = jnp.floor(x * inv + 0.5)
    a = (x - k * n) * (inv * (math.pi / 2))
    q = k.astype(jnp.int32)
    z = a * a
    s = a + a * z * (-1.6666654611e-1 + z * (8.3321608736e-3 + z * -1.9515295891e-4))
    c = 1.0 - 0.5 * z + z * z * (
        4.166664568298827e-2 + z * (-1.388731625493765e-3 + z * 2.443315711809948e-5)
    )
    odd = (q & 1) == 1
    cos, sin = jnp.where(odd, s, c), jnp.where(odd, c, s)
    cos = jnp.where(((q + 1) & 2) == 2, -cos, cos)
    sin = jnp.where((q & 2) == 2, -sin, sin)
    return cos, sin


def kernel(
    chips, cores, levs, quarter,
    spec_hbm, leg_ref, order_hbm, nlon_hbm, rows_hbm, out_ref,
    spec_ref, order_s, nlon_s, order_v, lbuf, xbuf, zbuf, send1, recv1, send2, recv2, table, twist, mixed, gbuf, vbuf,
    in_sem, leg_sem, s1_sem, r1_sem, s2_sem, r2_sem,
):
    slots, half, width = leg_ref.shape
    fields = spec_ref.shape[1]
    total = fields * levs
    w = lax.axis_index("wave")
    x = lax.axis_index("lev")
    chip, core = w // cores, lax.rem(w, cores)

    inputs = [
        pltpu.make_async_copy(src, dst, in_sem.at[i])
        for i, (src, dst) in enumerate(
            [(spec_hbm, spec_ref), (order_hbm, order_s), (nlon_hbm, nlon_s), (rows_hbm, order_v)]
        )
    ]
    cuts = [slots * i // GROUPS for i in range(GROUPS + 1)]
    legs = [
        pltpu.make_async_copy(leg_ref.at[a:b], lbuf.at[a:b], leg_sem.at[i])
        for i, (a, b) in enumerate(zip(cuts, cuts[1:]))
    ]

    side = math.isqrt(chips)
    y, z = chip // side, lax.rem(chip, side)
    ys = [lax.rem(y + d, side) for d in range(side)]
    zs = [lax.rem(z + d, side) for d in range(side)]
    cs = [lax.rem(core + d, cores) for d in range(cores)]
    xs = [lax.rem(x + d, levs) for d in range(levs)]

    def hops(d, n):
        return min(d, n - d)

    def far_first(n1, n2, weight):
        pairs = [(d, e) for d in range(n1) for e in range(n2) if d or e]
        return sorted(pairs, key=lambda d: -hops(d[0], n1) - weight * hops(d[1], n2))

    mates = [(ys[d], cs[e]) for d, e in far_first(side, cores, 0.1)]
    rest = [(zs[d], xs[e]) for d, e in far_first(side, levs, 1)]

    def mate_id(there):
        return ((there[0] * side + z) * cores + there[1], x)

    def rest_id(there):
        return ((y * side + there[0]) * cores + core, there[1])

    barrier = pltpu.get_barrier_semaphore()
    for i, there in enumerate([rest_id(r) for r in rest] + [mate_id(r) for r in mates]):
        if i == side:
            for copy in inputs + legs:
                copy.start()
        pl.semaphore_signal(barrier, inc=1, device_id=there, device_id_type=MESH)
    for copy in inputs:
        copy.wait()

    offset = iota((1, width), 1)
    parity = (1 - 2 * lax.rem(offset, 2)).astype(F32)
    zbuf[...] = jnp.zeros_like(zbuf)
    n = 2 * fields
    for p in range(slots):
        live = offset < width - order_s[w * slots + p]
        for f in range(fields):
            coeffs = jnp.where(live, spec_ref[p, f].astype(F32), 0.0)
            xbuf[p, 2 * f : 2 * f + 2] = coeffs
            xbuf[p, 8 + 2 * f : 8 + 2 * f + 2] = coeffs * parity
    for copy, a, b in zip(legs, cuts, cuts[1:]):
        copy.wait()
        for p in range(a, b):
            sums = lax.dot_general(xbuf[p].astype(BF16), lbuf[p], NT, preferred_element_type=F32)
            zbuf[n * p : n * p + n] = sums[0:n]
            zbuf[HALF + n * p : HALF + n * p + n] = sums[8 : 8 + n]

    total_mates = side * cores
    values = zbuf[...].astype(BF16).astype(F32)
    north = iota((LANES, half), 0) < HALF
    pair = jnp.concatenate([jnp.where(north, values, 0.0), jnp.where(north, 0.0, values)], 1).astype(BF16)
    r, g = iota((half, 2 * half), 0), iota((half, 2 * half), 1)
    h = (r // total_mates * side + lax.rem(r, side)) * cores + lax.rem(r // side, cores)
    route = ((g == h) | ((g == 2 * half - 1 - h) & (g >= half))).astype(F32).astype(BF16)
    send1[...] = lax.dot_general(route, pair, NT, preferred_element_type=F32)

    pl.semaphore_wait(barrier, len(mates) + len(rest))

    def block(i):
        return pl.ds(pl.multiple_of(i * side, side), side)

    def remote(src, dst, sems, there):
        return pltpu.make_async_remote_copy(
            src_ref=src, dst_ref=dst, send_sem=sems[0], recv_sem=sems[1], device_id=there, device_id_type=MESH
        )

    own = y * cores + core
    for there in mates:
        remote(send1.at[block(there[0] * cores + there[1])], recv1.at[block(own)], (s1_sem, r1_sem), mate_id(there)).start()
    recv1[block(own)] = send1[block(own)]

    rows_v = order_v.shape[0]
    lane = iota((1, half), 1)
    device = (lax.rem(lane, total_mates) // cores * side + lane // total_mates) * cores + lax.rem(lane, cores)
    high, low = (order_v[...] // 256).astype(F32).astype(BF16), lax.rem(order_v[...], 256).astype(F32).astype(BF16)
    for p in range(slots):
        place = device * slots + p
        pick = (iota((order_v.shape[1], half), 0) == lax.rem(place, order_v.shape[1])).astype(F32).astype(BF16)
        both = 256.0 * jnp.dot(high, pick, preferred_element_type=F32) + jnp.dot(low, pick, preferred_element_type=F32)
        row = iota((rows_v, half), 0) == place // order_v.shape[1]
        vbuf[p : p + 1] = jnp.sum(jnp.where(row, both, 0.0), 0, keepdims=True)

    counts = [nlon_s[w].astype(F32), nlon_s[half - 1 - w].astype(F32)]
    inverse = [1.0 / jnp.full((1, half), n, F32) for n in counts]
    fine = iota((STEP, half), 0).astype(F32)
    for ns in range(2):
        n, inv = counts[ns], inverse[ns]
        for p in range(slots):
            m = vbuf[p : p + 1]
            cb, sb = sincos(m * fine, n, inv, False)
            ca, sa = sincos(m * (STEP * fine), n, inv, False)
            for a in range(SPAN // STEP):
                c1, s1 = ca[a : a + 1], sa[a : a + 1]
                here = pl.ds(a * STEP, STEP)
                table[ns, here, p * half : (p + 1) * half] = (c1 * cb - s1 * sb).astype(BF16)
                table[ns, here, (slots + p) * half : (slots + p + 1) * half] = (-(c1 * sb) - s1 * cb).astype(BF16)

    most = pl.ds(0, side * (total_mates - 1))
    first_all = remote(send1.at[most], recv1.at[most], (s1_sem, r1_sem), mate_id(mates[0]))
    first_all.wait_recv()
    for i in range(side):
        send2[i] = recv1[pl.ds(i, total_mates, stride=side)].astype(BF16)
    for there in rest:
        remote(send2.at[there[0]], recv2.at[x * side + z], (s2_sem, r2_sem), rest_id(there)).start()
    recv2[x * side + z] = send2[z]

    first = x * quarter
    spans = pl.cdiv(quarter, SPAN)
    starts = (first + SPAN * iota((8, half), 0)).astype(F32)
    for ns in range(2):
        n, inv = counts[ns], inverse[ns]
        for p in range(slots):
            m = vbuf[p : p + 1]
            weight = jnp.where(2.0 * m < n, jnp.where(m == 0.0, 1.0, 2.0), 0.0)
            ct, st = sincos(m * starts, n, inv, True)
            twist[ns, p, 0] = ct * weight
            twist[ns, p, 1] = st * weight

    f16 = iota((STEP, LANES), 0)
    gap = iota((STEP, LANES), 1) - 2 * f16
    parts = [(f16 >= fields * v) & (f16 < fields * (v + 1)) for v in range(levs)]
    picks = []
    for ns in range(2):
        for c in range(2):
            for p in range(slots):
                at = HALF * ns + 2 * fields * p + c
                picks.append(
                    jnp.concatenate(
                        [((gap == at - 2 * fields * v) & parts[v]).astype(F32) for v in range(levs)], 1
                    ).astype(BF16)
                )
    choice = jnp.concatenate(picks, 0)

    most = pl.ds(0, side * levs - 1)
    second_all = remote(recv2.at[most], recv2.at[most], (s2_sem, r2_sem), rest_id(rest[0]))
    second_all.wait_recv()
    arrived = jnp.concatenate(
        [recv2[v * side : (v + 1) * side].reshape(half, LANES) for v in range(levs)], 1
    )
    mixed[...] = lax.dot_general(choice, arrived, NT, preferred_element_type=F32)

    for ns in range(2):
        for p in range(slots):
            at = STEP * (2 * slots * ns + p)
            re, im = mixed[at : at + STEP], mixed[at + STEP * slots : at + STEP * slots + STEP]
            for s in range(spans):
                ct, st = twist[ns, p, 0, s : s + 1], twist[ns, p, 1, s : s + 1]
                here = pl.ds(s * STEP, STEP)
                gbuf[ns, here, p * half : (p + 1) * half] = (re * ct - im * st).astype(BF16)
                gbuf[ns, here, (slots + p) * half : (slots + p + 1) * half] = (re * st + im * ct).astype(BF16)
        grid = lax.dot_general(gbuf[ns], table[ns], NT, preferred_element_type=F32)
        for s in range(spans):
            size = min(SPAN, quarter - s * SPAN)
            place = first + s * SPAN + iota((total, size), 1)
            keep = place < nlon_s[w if ns == 0 else half - 1 - w]
            out_ref[ns * total : (ns + 1) * total, s * SPAN : s * SPAN + size] = jnp.where(
                keep, grid[s * STEP : s * STEP + total, :size], 0.0
            )
    first_all.wait_send()
    second_all.wait_send()


def shards(spectral, legendre, wave_order, nlon):
    slots, half, width = legendre.shape
    fields = spectral.shape[1]
    waves, levs = lax.axis_size("wave"), lax.axis_size("lev")
    cores = 2
    chips = waves // cores
    side = math.isqrt(chips)
    quarter = (4 * width + 16) // levs
    spans = pl.cdiv(quarter, SPAN)
    hbm = pl.BlockSpec(memory_space=pltpu.HBM)
    dma = pltpu.SemaphoreType.DMA
    order_rows = wave_order.reshape(-1, min(LANES, wave_order.shape[0] // slots))
    grid = pl.pallas_call(
        functools.partial(kernel, chips, cores, levs, quarter),
        out_shape=pltpu.VMEM((2 * fields * levs, quarter), F32),
        in_specs=[hbm] * 5,
        out_specs=pl.BlockSpec(memory_space=pltpu.VMEM),
        scratch_shapes=[
            pltpu.VMEM(spectral.shape, BF16),
            pltpu.SMEM(wave_order.shape, jnp.int32),
            pltpu.SMEM(nlon.shape, jnp.int32),
            pltpu.VMEM(order_rows.shape, jnp.int32),
            pltpu.VMEM((slots, half, width), BF16),
            pltpu.VMEM((slots, 16, width), F32),
            pltpu.VMEM((LANES, half), F32),
            pltpu.VMEM((half, LANES), F32),
            pltpu.VMEM((half, LANES), F32),
            pltpu.VMEM((side, side * cores, LANES), BF16),
            pltpu.VMEM((levs * side, side * cores, LANES), BF16),
            pltpu.VMEM((2, SPAN, 2 * slots * half), BF16),
            pltpu.VMEM((2, slots, 2, 8, half), F32),
            pltpu.VMEM((4 * slots * STEP, half), F32),
            pltpu.VMEM((2, spans * STEP, 2 * slots * half), BF16),
            pltpu.VMEM((16, half), F32),
            dma((4,)),
            dma((GROUPS,)),
            dma,
            dma,
            dma,
            dma,
        ],
        compiler_params=pltpu.CompilerParams(
            collective_id=0, has_side_effects=True, vmem_limit_bytes=64 * 1024 * 1024 - 400000
        ),
    )(spectral, legendre, wave_order, nlon, order_rows)
    return jnp.transpose(grid.reshape(2, fields * levs, quarter), (1, 0, 2))


def solution(mesh):
    placed = (P("wave", "lev", None, None), P("wave", None, None), P(), P())
    return jax.shard_map(
        shards, mesh=mesh, in_specs=placed, out_specs=P(None, "wave", "lev"), check_vma=False
    )
```

```python
import functools
import math

import jax
import jax.numpy as jnp
from jax import lax
from jax.experimental import pallas as pl
from jax.experimental.pallas import tpu as pltpu
from jax.sharding import PartitionSpec as P

MESH = pl.DeviceIdType.MESH
F32 = jnp.float32
BF16 = jnp.bfloat16
LANES = 128
HALF = LANES // 2
SPAN = 128
GROUPS = 2
STEP = 16
NT = (((1,), (1,)), ((), ()))


def iota(shape, dim):
    return lax.broadcasted_iota(jnp.int32, shape, dim)


def sincos(x, n, inv, far):
    if far:
        x = x - jnp.floor(x * inv + 0.5) * n
    x = 4.0 * x
    k = jnp.floor(x * inv + 0.5)
    a = (x - k * n) * (inv * (math.pi / 2))
    q = k.astype(jnp.int32)
    z = a * a
    s = a + a * z * (-1.6666654611e-1 + z * (8.3321608736e-3 + z * -1.9515295891e-4))
    c = 1.0 - 0.5 * z + z * z * (
        4.166664568298827e-2 + z * (-1.388731625493765e-3 + z * 2.443315711809948e-5)
    )
    odd = (q & 1) == 1
    cos, sin = jnp.where(odd, s, c), jnp.where(odd, c, s)
    cos = jnp.where(((q + 1) & 2) == 2, -cos, cos)
    sin = jnp.where((q & 2) == 2, -sin, sin)
    return cos, sin


def kernel(
    chips, cores, levs, quarter,
    spec_hbm, leg_ref, order_hbm, nlon_hbm, rows_hbm, out_ref,
    spec_ref, order_s, nlon_s, order_v, lbuf, xbuf, zbuf, send1, recv1, send2, recv2, table, twist, mixed, gbuf, vbuf,
    in_sem, leg_sem, s1_sem, r1_sem, s2_sem, r2_sem,
):
    slots, half, width = leg_ref.shape
    fields = spec_ref.shape[1]
    total = fields * levs
    w = lax.axis_index("wave")
    x = lax.axis_index("lev")
    chip, core = w // cores, lax.rem(w, cores)

    inputs = [
        pltpu.make_async_copy(src, dst, in_sem.at[i])
        for i, (src, dst) in enumerate(
            [(spec_hbm, spec_ref), (order_hbm, order_s), (nlon_hbm, nlon_s), (rows_hbm, order_v)]
        )
    ]
    cuts = [slots * i // GROUPS for i in range(GROUPS + 1)]
    legs = [
        pltpu.make_async_copy(leg_ref.at[a:b], lbuf.at[a:b], leg_sem.at[i])
        for i, (a, b) in enumerate(zip(cuts, cuts[1:]))
    ]

    side = math.isqrt(chips)
    z, y = chip // side, lax.rem(chip, side)
    cs = [lax.rem(core + d, cores) for d in range(cores)]
    xs = [lax.rem(x + d, levs) for d in range(levs)]

    def hops(d, n):
        return min(d, n - d)

    def others(mine, n):
        return [k + (mine <= k).astype(jnp.int32) for k in range(n - 1)]

    far_x = sorted(range(levs), key=lambda d: -hops(d, levs))
    mates = [(k, c) for k in others(y, side) for c in cs] + [(y, c) for c in cs[1:]]
    rest = [(k, xs[d]) for k in others(z, side) for d in far_x] + [(z, xs[d]) for d in far_x if d]

    def mate_id(there):
        return ((z * side + there[0]) * cores + there[1], x)

    def rest_id(there):
        return ((there[0] * side + y) * cores + core, there[1])

    barrier = pltpu.get_barrier_semaphore()
    for copy in inputs[:2] + legs + inputs[2:]:
        copy.start()
    for there in [mate_id(r) for r in mates] + [rest_id(r) for r in rest]:
        pl.semaphore_signal(barrier, inc=1, device_id=there, device_id_type=MESH)
    for copy in inputs[:2]:
        copy.wait()

    offset = iota((1, width), 1)
    parity = (1 - 2 * lax.rem(offset, 2)).astype(F32)
    zbuf[...] = jnp.zeros_like(zbuf)
    n = 2 * fields
    for p in range(slots):
        live = offset < width - order_s[w * slots + p]
        for f in range(fields):
            coeffs = jnp.where(live, spec_ref[p, f].astype(F32), 0.0)
            xbuf[p, 2 * f : 2 * f + 2] = coeffs
            xbuf[p, 8 + 2 * f : 8 + 2 * f + 2] = coeffs * parity
    for copy, a, b in zip(legs, cuts, cuts[1:]):
        copy.wait()
        for p in range(a, b):
            sums = lax.dot_general(xbuf[p].astype(BF16), lbuf[p], NT, preferred_element_type=F32)
            zbuf[n * p : n * p + n] = sums[0:n]
            zbuf[HALF + n * p : HALF + n * p + n] = sums[8 : 8 + n]

    total_mates = side * cores
    values = zbuf[...].astype(BF16).astype(F32)
    north = iota((LANES, half), 0) < HALF
    pair = jnp.concatenate([jnp.where(north, values, 0.0), jnp.where(north, 0.0, values)], 1).astype(BF16)
    r, g = iota((half, 2 * half), 0), iota((half, 2 * half), 1)
    h = (r // total_mates + lax.rem(r, side) * side) * cores + lax.rem(r // side, cores)
    route = ((g == h) | ((g == 2 * half - 1 - h) & (g >= half))).astype(F32).astype(BF16)
    send1[...] = lax.dot_general(route, pair, NT, preferred_element_type=F32)

    pl.semaphore_wait(barrier, len(mates) + len(rest))

    def block(i):
        return pl.ds(pl.multiple_of(i * side, side), side)

    def remote(src, dst, sems, there):
        return pltpu.make_async_remote_copy(
            src_ref=src, dst_ref=dst, send_sem=sems[0], recv_sem=sems[1], device_id=there, device_id_type=MESH
        )

    own = y * cores + core
    for there in mates:
        remote(send1.at[block(there[0] * cores + there[1])], recv1.at[block(own)], (s1_sem, r1_sem), mate_id(there)).start()
    recv1[block(own)] = send1[block(own)]

    for copy in inputs[2:]:
        copy.wait()

    rows_v = order_v.shape[0]
    lane = iota((1, half), 1)
    device = (lax.rem(lane, total_mates) // cores + lane // total_mates * side) * cores + lax.rem(lane, cores)
    high, low = (order_v[...] // 256).astype(F32).astype(BF16), lax.rem(order_v[...], 256).astype(F32).astype(BF16)
    for p in range(slots):
        place = device * slots + p
        pick = (iota((order_v.shape[1], half), 0) == lax.rem(place, order_v.shape[1])).astype(F32).astype(BF16)
        both = 256.0 * jnp.dot(high, pick, preferred_element_type=F32) + jnp.dot(low, pick, preferred_element_type=F32)
        row = iota((rows_v, half), 0) == place // order_v.shape[1]
        vbuf[p : p + 1] = jnp.sum(jnp.where(row, both, 0.0), 0, keepdims=True)

    counts = [nlon_s[w].astype(F32), nlon_s[half - 1 - w].astype(F32)]
    inverse = [1.0 / jnp.full((1, half), n, F32) for n in counts]
    fine = iota((STEP, half), 0).astype(F32)
    for ns in range(2):
        n, inv = counts[ns], inverse[ns]
        for p in range(slots):
            m = vbuf[p : p + 1]
            cb, sb = sincos(m * fine, n, inv, False)
            ca, sa = sincos(m * (STEP * fine), n, inv, False)
            for a in range(SPAN // STEP):
                c1, s1 = ca[a : a + 1], sa[a : a + 1]
                here = pl.ds(a * STEP, STEP)
                table[ns, here, p * half : (p + 1) * half] = (c1 * cb - s1 * sb).astype(BF16)
                table[ns, here, (slots + p) * half : (slots + p + 1) * half] = (-(c1 * sb) - s1 * cb).astype(BF16)

    most = pl.ds(0, side * (total_mates - 1))
    first_all = remote(send1.at[most], recv1.at[most], (s1_sem, r1_sem), mate_id(mates[0]))
    first_all.wait_recv()
    for i in range(side):
        send2[i] = recv1[pl.ds(i, total_mates, stride=side)].astype(BF16)
    for there in rest:
        remote(send2.at[there[0]], recv2.at[x * side + z], (s2_sem, r2_sem), rest_id(there)).start()
    recv2[x * side + z] = send2[z]

    first = x * quarter
    spans = pl.cdiv(quarter, SPAN)
    starts = (first + SPAN * iota((16, half), 0)).astype(F32)
    for ns in range(2):
        n, inv = counts[ns], inverse[ns]
        for p in range(slots):
            m = vbuf[p : p + 1]
            weight = jnp.where(2.0 * m < n, jnp.where(m == 0.0, 1.0, 2.0), 0.0)
            ct, st = sincos(m * starts, n, inv, True)
            twist[ns, p, 0] = ct * weight
            twist[ns, p, 1] = st * weight

    f16 = iota((STEP, LANES), 0)
    gap = iota((STEP, LANES), 1) - 2 * f16
    parts = [(f16 >= fields * v) & (f16 < fields * (v + 1)) for v in range(levs)]
    picks = []
    for ns in range(2):
        for c in range(2):
            for p in range(slots):
                at = HALF * ns + 2 * fields * p + c
                picks.append(
                    jnp.concatenate(
                        [((gap == at - 2 * fields * v) & parts[v]).astype(F32) for v in range(levs)], 1
                    ).astype(BF16)
                )
    choice = jnp.concatenate(picks, 0)

    most = pl.ds(0, side * levs - 1)
    second_all = remote(recv2.at[most], recv2.at[most], (s2_sem, r2_sem), rest_id(rest[0]))
    second_all.wait_recv()
    arrived = jnp.concatenate(
        [recv2[v * side : (v + 1) * side].reshape(half, LANES) for v in range(levs)], 1
    )
    mixed[...] = lax.dot_general(choice, arrived, NT, preferred_element_type=F32)

    for ns in range(2):
        for p in range(slots):
            at = STEP * (2 * slots * ns + p)
            re, im = mixed[at : at + STEP], mixed[at + STEP * slots : at + STEP * slots + STEP]
            for s in range(spans):
                ct, st = twist[ns, p, 0, s : s + 1], twist[ns, p, 1, s : s + 1]
                here = pl.ds(s * STEP, STEP)
                gbuf[ns, here, p * half : (p + 1) * half] = (re * ct - im * st).astype(BF16)
                gbuf[ns, here, (slots + p) * half : (slots + p + 1) * half] = (re * st + im * ct).astype(BF16)
        grid = lax.dot_general(gbuf[ns], table[ns], NT, preferred_element_type=F32)
        for s in range(spans):
            size = min(SPAN, quarter - s * SPAN)
            place = first + s * SPAN + iota((total, size), 1)
            keep = place < nlon_s[w if ns == 0 else half - 1 - w]
            out_ref[:, ns, s * SPAN : s * SPAN + size] = jnp.where(
                keep, grid[s * STEP : s * STEP + total, :size], 0.0
            )
    first_all.wait_send()
    second_all.wait_send()


def shards(spectral, legendre, wave_order, nlon):
    slots, half, width = legendre.shape
    fields = spectral.shape[1]
    waves, levs = lax.axis_size("wave"), lax.axis_size("lev")
    cores = 2
    chips = waves // cores
    side = math.isqrt(chips)
    quarter = (4 * width + 16) // levs
    spans = pl.cdiv(quarter, SPAN)
    hbm = pl.BlockSpec(memory_space=pltpu.HBM)
    dma = pltpu.SemaphoreType.DMA
    order_rows = wave_order.reshape(-1, min(LANES, wave_order.shape[0] // slots))
    grid = pl.pallas_call(
        functools.partial(kernel, chips, cores, levs, quarter),
        out_shape=pltpu.VMEM((fields * levs, 2, quarter), F32),
        in_specs=[hbm] * 5,
        out_specs=pl.BlockSpec(memory_space=pltpu.VMEM),
        scratch_shapes=[
            pltpu.VMEM(spectral.shape, BF16),
            pltpu.SMEM(wave_order.shape, jnp.int32),
            pltpu.SMEM(nlon.shape, jnp.int32),
            pltpu.VMEM(order_rows.shape, jnp.int32),
            pltpu.VMEM((slots, half, width), BF16),
            pltpu.VMEM((slots, 16, width), F32),
            pltpu.VMEM((LANES, half), F32),
            pltpu.VMEM((half, LANES), F32),
            pltpu.VMEM((half, LANES), F32),
            pltpu.VMEM((side, side * cores, LANES), BF16),
            pltpu.VMEM((levs * side, side * cores, LANES), BF16),
            pltpu.VMEM((2, SPAN, 2 * slots * half), BF16),
            pltpu.VMEM((2, slots, 2, 16, half), F32),
            pltpu.VMEM((4 * slots * STEP, half), F32),
            pltpu.VMEM((2, spans * STEP, 2 * slots * half), BF16),
            pltpu.VMEM((16, half), F32),
            dma((4,)),
            dma((GROUPS,)),
            dma,
            dma,
            dma,
            dma,
        ],
        compiler_params=pltpu.CompilerParams(
            collective_id=0, has_side_effects=True, vmem_limit_bytes=64 * 1024 * 1024 - 400000
        ),
    )(spectral, legendre, wave_order, nlon, order_rows)
    return grid


def solution(mesh):
    placed = (P("wave", "lev", None, None), P("wave", None, None), P(), P())
    return jax.shard_map(
        shards, mesh=mesh, in_specs=placed, out_specs=P(None, "wave", "lev"), check_vma=False
    )
```

```python
import functools
import math

import jax
import jax.numpy as jnp
from jax import lax
from jax.experimental import pallas as pl
from jax.experimental.pallas import tpu as pltpu
from jax.sharding import PartitionSpec as P

MESH = pl.DeviceIdType.MESH
F32 = jnp.float32
BF16 = jnp.bfloat16
LANES = 128
HALF = LANES // 2
SPAN = 128
GROUPS = 2
STEP = 16
NT = (((1,), (1,)), ((), ()))


def iota(shape, dim):
    return lax.broadcasted_iota(jnp.int32, shape, dim)


def sincos(x, n, inv, far):
    if far:
        x = x - jnp.floor(x * inv + 0.5) * n
    x = 4.0 * x
    k = jnp.floor(x * inv + 0.5)
    a = (x - k * n) * (inv * (math.pi / 2))
    q = k.astype(jnp.int32)
    z = a * a
    s = a + a * z * (-1.6666654611e-1 + z * (8.3321608736e-3 + z * -1.9515295891e-4))
    c = 1.0 - 0.5 * z + z * z * (
        4.166664568298827e-2 + z * (-1.388731625493765e-3 + z * 2.443315711809948e-5)
    )
    odd = (q & 1) == 1
    cos, sin = jnp.where(odd, s, c), jnp.where(odd, c, s)
    cos = jnp.where(((q + 1) & 2) == 2, -cos, cos)
    sin = jnp.where((q & 2) == 2, -sin, sin)
    return cos, sin


def kernel(
    chips, cores, levs, quarter,
    spec_hbm, leg_ref, order_hbm, nlon_hbm, rows_hbm, out_ref,
    spec_ref, order_s, nlon_s, order_v, lbuf, xbuf, zbuf, send1, recv1, send2, recv2, table, twist, mixed, gbuf, vbuf,
    in_sem, leg_sem, s1_sem, r1_sem, s2_sem, r2_sem,
):
    slots, half, width = leg_ref.shape
    fields = spec_ref.shape[1]
    total = fields * levs
    w = lax.axis_index("wave")
    x = lax.axis_index("lev")
    chip, core = w // cores, lax.rem(w, cores)

    inputs = [
        pltpu.make_async_copy(src, dst, in_sem.at[i])
        for i, (src, dst) in enumerate(
            [(spec_hbm, spec_ref), (order_hbm, order_s), (nlon_hbm, nlon_s), (rows_hbm, order_v)]
        )
    ]
    cuts = [slots * i // GROUPS for i in range(GROUPS + 1)]
    legs = [
        pltpu.make_async_copy(leg_ref.at[a:b], lbuf.at[a:b], leg_sem.at[i])
        for i, (a, b) in enumerate(zip(cuts, cuts[1:]))
    ]

    side = math.isqrt(chips)
    z, y = chip // side, lax.rem(chip, side)
    cs = [lax.rem(core + d, cores) for d in range(cores)]
    xs = [lax.rem(x + d, levs) for d in range(levs)]

    def hops(d, n):
        return min(d, n - d)

    def others(mine, n):
        return [k + (mine <= k).astype(jnp.int32) for k in range(n - 1)]

    far_x = sorted(range(levs), key=lambda d: -hops(d, levs))
    mates = [(k, c) for k in others(y, side) for c in cs[::-1]] + [(y, c) for c in cs[1:]]
    rest = [(k, xs[d]) for k in others(z, side) for d in far_x] + [(z, xs[d]) for d in far_x if d]

    def mate_id(there):
        return ((z * side + there[0]) * cores + there[1], x)

    def rest_id(there):
        return ((there[0] * side + y) * cores + core, there[1])

    barrier = pltpu.get_barrier_semaphore()
    for copy in inputs[:2] + legs + inputs[2:]:
        copy.start()
    for there in [mate_id(r) for r in mates] + [rest_id(r) for r in rest]:
        pl.semaphore_signal(barrier, inc=1, device_id=there, device_id_type=MESH)
    for copy in inputs[:2]:
        copy.wait()

    offset = iota((1, width), 1)
    parity = (1 - 2 * lax.rem(offset, 2)).astype(F32)
    zbuf[...] = jnp.zeros_like(zbuf)
    n = 2 * fields
    for p in range(slots):
        live = offset < width - order_s[w * slots + p]
        for f in range(fields):
            coeffs = jnp.where(live, spec_ref[p, f].astype(F32), 0.0)
            xbuf[p, 2 * f : 2 * f + 2] = coeffs
            xbuf[p, 8 + 2 * f : 8 + 2 * f + 2] = coeffs * parity
    for copy, a, b in zip(legs, cuts, cuts[1:]):
        copy.wait()
        for p in range(a, b):
            sums = lax.dot_general(xbuf[p].astype(BF16), lbuf[p], NT, preferred_element_type=F32)
            zbuf[n * p : n * p + n] = sums[0:n]
            zbuf[HALF + n * p : HALF + n * p + n] = sums[8 : 8 + n]

    total_mates = side * cores
    values = zbuf[...].astype(BF16).astype(F32)
    north = iota((LANES, half), 0) < HALF
    pair = jnp.concatenate([jnp.where(north, values, 0.0), jnp.where(north, 0.0, values)], 1).astype(BF16)
    r, g = iota((half, 2 * half), 0), iota((half, 2 * half), 1)
    h = (r // total_mates + lax.rem(r, side) * side) * cores + lax.rem(r // side, cores)
    route = ((g == h) | ((g == 2 * half - 1 - h) & (g >= half))).astype(F32).astype(BF16)
    send1[...] = lax.dot_general(route, pair, NT, preferred_element_type=F32)

    pl.semaphore_wait(barrier, len(mates) + len(rest))

    def block(i):
        return pl.ds(pl.multiple_of(i * side, side), side)

    def remote(src, dst, sems, there):
        return pltpu.make_async_remote_copy(
            src_ref=src, dst_ref=dst, send_sem=sems[0], recv_sem=sems[1], device_id=there, device_id_type=MESH
        )

    own = y * cores + core
    for there in mates:
        remote(send1.at[block(there[0] * cores + there[1])], recv1.at[block(own)], (s1_sem, r1_sem), mate_id(there)).start()
    recv1[block(own)] = send1[block(own)]

    for copy in inputs[2:]:
        copy.wait()

    rows_v = order_v.shape[0]
    lane = iota((1, half), 1)
    device = (lax.rem(lane, total_mates) // cores + lane // total_mates * side) * cores + lax.rem(lane, cores)
    high, low = (order_v[...] // 256).astype(F32).astype(BF16), lax.rem(order_v[...], 256).astype(F32).astype(BF16)
    for p in range(slots):
        place = device * slots + p
        pick = (iota((order_v.shape[1], half), 0) == lax.rem(place, order_v.shape[1])).astype(F32).astype(BF16)
        both = 256.0 * jnp.dot(high, pick, preferred_element_type=F32) + jnp.dot(low, pick, preferred_element_type=F32)
        row = iota((rows_v, half), 0) == place // order_v.shape[1]
        vbuf[p : p + 1] = jnp.sum(jnp.where(row, both, 0.0), 0, keepdims=True)

    counts = [nlon_s[w].astype(F32), nlon_s[half - 1 - w].astype(F32)]
    inverse = [1.0 / jnp.full((1, half), n, F32) for n in counts]
    fine = iota((STEP, half), 0).astype(F32)
    for ns in range(2):
        n, inv = counts[ns], inverse[ns]
        for p in range(slots):
            m = vbuf[p : p + 1]
            cb, sb = sincos(m * fine, n, inv, False)
            ca, sa = sincos(m * (STEP * fine), n, inv, False)
            for a in range(SPAN // STEP):
                c1, s1 = ca[a : a + 1], sa[a : a + 1]
                here = pl.ds(a * STEP, STEP)
                table[ns, here, p * half : (p + 1) * half] = (c1 * cb - s1 * sb).astype(BF16)
                table[ns, here, (slots + p) * half : (slots + p + 1) * half] = (-(c1 * sb) - s1 * cb).astype(BF16)

    most = pl.ds(0, side * (total_mates - 1))
    first_all = remote(send1.at[most], recv1.at[most], (s1_sem, r1_sem), mate_id(mates[0]))
    first_all.wait_recv()
    for i in range(side):
        send2[i] = recv1[pl.ds(i, total_mates, stride=side)].astype(BF16)
    for there in rest:
        remote(send2.at[there[0]], recv2.at[x * side + z], (s2_sem, r2_sem), rest_id(there)).start()
    recv2[x * side + z] = send2[z]

    first = x * quarter
    spans = pl.cdiv(quarter, SPAN)
    starts = (first + SPAN * iota((16, half), 0)).astype(F32)
    for ns in range(2):
        n, inv = counts[ns], inverse[ns]
        for p in range(slots):
            m = vbuf[p : p + 1]
            weight = jnp.where(2.0 * m < n, jnp.where(m == 0.0, 1.0, 2.0), 0.0)
            ct, st = sincos(m * starts, n, inv, True)
            twist[ns, p, 0] = ct * weight
            twist[ns, p, 1] = st * weight

    f16 = iota((STEP, LANES), 0)
    gap = iota((STEP, LANES), 1) - 2 * f16
    parts = [(f16 >= fields * v) & (f16 < fields * (v + 1)) for v in range(levs)]
    picks = []
    for ns in range(2):
        for c in range(2):
            for p in range(slots):
                at = HALF * ns + 2 * fields * p + c
                picks.append(
                    jnp.concatenate(
                        [((gap == at - 2 * fields * v) & parts[v]).astype(F32) for v in range(levs)], 1
                    ).astype(BF16)
                )
    choice = jnp.concatenate(picks, 0)

    most = pl.ds(0, side * levs - 1)
    second_all = remote(recv2.at[most], recv2.at[most], (s2_sem, r2_sem), rest_id(rest[0]))
    second_all.wait_recv()
    arrived = jnp.concatenate(
        [recv2[v * side : (v + 1) * side].reshape(half, LANES) for v in range(levs)], 1
    )
    mixed[...] = lax.dot_general(choice, arrived, NT, preferred_element_type=F32)

    for ns in range(2):
        for p in range(slots):
            at = STEP * (2 * slots * ns + p)
            re, im = mixed[at : at + STEP], mixed[at + STEP * slots : at + STEP * slots + STEP]
            for s in range(spans):
                ct, st = twist[ns, p, 0, s : s + 1], twist[ns, p, 1, s : s + 1]
                here = pl.ds(s * STEP, STEP)
                gbuf[ns, here, p * half : (p + 1) * half] = (re * ct - im * st).astype(BF16)
                gbuf[ns, here, (slots + p) * half : (slots + p + 1) * half] = (re * st + im * ct).astype(BF16)
        grid = lax.dot_general(gbuf[ns], table[ns], NT, preferred_element_type=F32)
        for s in range(spans):
            size = min(SPAN, quarter - s * SPAN)
            place = first + s * SPAN + iota((total, size), 1)
            keep = place < nlon_s[w if ns == 0 else half - 1 - w]
            out_ref[:, ns, s * SPAN : s * SPAN + size] = jnp.where(
                keep, grid[s * STEP : s * STEP + total, :size], 0.0
            )
    first_all.wait_send()
    second_all.wait_send()


def shards(spectral, legendre, wave_order, nlon):
    slots, half, width = legendre.shape
    fields = spectral.shape[1]
    waves, levs = lax.axis_size("wave"), lax.axis_size("lev")
    cores = 2
    chips = waves // cores
    side = math.isqrt(chips)
    quarter = (4 * width + 16) // levs
    spans = pl.cdiv(quarter, SPAN)
    hbm = pl.BlockSpec(memory_space=pltpu.HBM)
    dma = pltpu.SemaphoreType.DMA
    order_rows = wave_order.reshape(-1, min(LANES, wave_order.shape[0] // slots))
    grid = pl.pallas_call(
        functools.partial(kernel, chips, cores, levs, quarter),
        out_shape=pltpu.VMEM((fields * levs, 2, quarter), F32),
        in_specs=[hbm] * 5,
        out_specs=pl.BlockSpec(memory_space=pltpu.VMEM),
        scratch_shapes=[
            pltpu.VMEM(spectral.shape, BF16),
            pltpu.SMEM(wave_order.shape, jnp.int32),
            pltpu.SMEM(nlon.shape, jnp.int32),
            pltpu.VMEM(order_rows.shape, jnp.int32),
            pltpu.VMEM((slots, half, width), BF16),
            pltpu.VMEM((slots, 16, width), F32),
            pltpu.VMEM((LANES, half), F32),
            pltpu.VMEM((half, LANES), F32),
            pltpu.VMEM((half, LANES), F32),
            pltpu.VMEM((side, side * cores, LANES), BF16),
            pltpu.VMEM((levs * side, side * cores, LANES), BF16),
            pltpu.VMEM((2, SPAN, 2 * slots * half), BF16),
            pltpu.VMEM((2, slots, 2, 16, half), F32),
            pltpu.VMEM((4 * slots * STEP, half), F32),
            pltpu.VMEM((2, spans * STEP, 2 * slots * half), BF16),
            pltpu.VMEM((16, half), F32),
            dma((4,)),
            dma((GROUPS,)),
            dma,
            dma,
            dma,
            dma,
        ],
        compiler_params=pltpu.CompilerParams(
            collective_id=0, has_side_effects=True, vmem_limit_bytes=64 * 1024 * 1024 - 400000
        ),
    )(spectral, legendre, wave_order, nlon, order_rows)
    return grid


def solution(mesh):
    placed = (P("wave", "lev", None, None), P("wave", None, None), P(), P())
    return jax.shard_map(
        shards, mesh=mesh, in_specs=placed, out_specs=P(None, "wave", "lev"), check_vma=False
    )
```

```python
import functools
import math

import jax
import jax.numpy as jnp
from jax import lax
from jax.experimental import pallas as pl
from jax.experimental.pallas import tpu as pltpu
from jax.sharding import PartitionSpec as P

MESH = pl.DeviceIdType.MESH
F32 = jnp.float32
BF16 = jnp.bfloat16
LANES = 128
HALF = LANES // 2
SPAN = 128
GROUPS = 2
STEP = 16
NT = (((1,), (1,)), ((), ()))


def iota(shape, dim):
    return lax.broadcasted_iota(jnp.int32, shape, dim)


def sincos(x, n, inv, far):
    if far:
        x = x - jnp.floor(x * inv + 0.5) * n
    x = 4.0 * x
    k = jnp.floor(x * inv + 0.5)
    a = (x - k * n) * (inv * (math.pi / 2))
    q = k.astype(jnp.int32)
    z = a * a
    s = a + a * z * (-1.6666654611e-1 + z * (8.3321608736e-3 + z * -1.9515295891e-4))
    c = 1.0 - 0.5 * z + z * z * (
        4.166664568298827e-2 + z * (-1.388731625493765e-3 + z * 2.443315711809948e-5)
    )
    odd = (q & 1) == 1
    cos, sin = jnp.where(odd, s, c), jnp.where(odd, c, s)
    cos = jnp.where(((q + 1) & 2) == 2, -cos, cos)
    sin = jnp.where((q & 2) == 2, -sin, sin)
    return cos, sin


def kernel(
    chips, cores, levs, quarter,
    spec_hbm, leg_ref, order_hbm, nlon_hbm, rows_hbm, out_ref,
    spec_ref, order_s, nlon_s, order_v, lbuf, xbuf, zbuf, send1, recv1, send2, recv2, table, twist, mixed, gbuf, vbuf,
    in_sem, leg_sem, s1_sem, r1_sem, s2_sem, r2_sem,
):
    slots, half, width = leg_ref.shape
    fields = spec_ref.shape[1]
    total = fields * levs
    w = lax.axis_index("wave")
    x = lax.axis_index("lev")
    chip, core = w // cores, lax.rem(w, cores)

    inputs = [
        pltpu.make_async_copy(src, dst, in_sem.at[i])
        for i, (src, dst) in enumerate(
            [(spec_hbm, spec_ref), (order_hbm, order_s), (nlon_hbm, nlon_s), (rows_hbm, order_v)]
        )
    ]
    cuts = [slots * i // GROUPS for i in range(GROUPS + 1)]
    legs = [
        pltpu.make_async_copy(leg_ref.at[a:b], lbuf.at[a:b], leg_sem.at[i])
        for i, (a, b) in enumerate(zip(cuts, cuts[1:]))
    ]

    side = math.isqrt(chips)
    z, y = chip // side, lax.rem(chip, side)
    cs = [lax.rem(core + d, cores) for d in range(cores)]
    xs = [lax.rem(x + d, levs) for d in range(levs)]

    def hops(d, n):
        return min(d, n - d)

    def others(mine, n):
        return [k + (mine <= k).astype(jnp.int32) for k in range(n - 1)]

    far_x = sorted(range(levs), key=lambda d: -hops(d, levs))
    mates = [(k, c) for k in others(y, side) for c in cs[::-1]] + [(y, c) for c in cs[1:]]
    rest = [(k, xs[d]) for k in others(z, side) for d in far_x] + [(z, xs[d]) for d in far_x if d]

    def mate_id(there):
        return ((z * side + there[0]) * cores + there[1], x)

    def rest_id(there):
        return ((there[0] * side + y) * cores + core, there[1])

    barrier = pltpu.get_barrier_semaphore()
    for i, there in enumerate([mate_id(r) for r in mates] + [rest_id(r) for r in rest]):
        if i == len(mates):
            for copy in inputs[:2] + legs + inputs[2:]:
                copy.start()
        pl.semaphore_signal(barrier, inc=1, device_id=there, device_id_type=MESH)
    for copy in inputs[:2]:
        copy.wait()

    offset = iota((1, width), 1)
    parity = (1 - 2 * lax.rem(offset, 2)).astype(F32)
    zbuf[...] = jnp.zeros_like(zbuf)
    n = 2 * fields
    for p in range(slots):
        live = offset < width - order_s[w * slots + p]
        for f in range(fields):
            coeffs = jnp.where(live, spec_ref[p, f].astype(F32), 0.0)
            xbuf[p, 2 * f : 2 * f + 2] = coeffs
            xbuf[p, 8 + 2 * f : 8 + 2 * f + 2] = coeffs * parity
    for copy, a, b in zip(legs, cuts, cuts[1:]):
        copy.wait()
        for p in range(a, b):
            sums = lax.dot_general(xbuf[p].astype(BF16), lbuf[p], NT, preferred_element_type=F32)
            zbuf[n * p : n * p + n] = sums[0:n]
            zbuf[HALF + n * p : HALF + n * p + n] = sums[8 : 8 + n]

    total_mates = side * cores
    values = zbuf[...].astype(BF16).astype(F32)
    north = iota((LANES, half), 0) < HALF
    pair = jnp.concatenate([jnp.where(north, values, 0.0), jnp.where(north, 0.0, values)], 1).astype(BF16)
    r, g = iota((half, 2 * half), 0), iota((half, 2 * half), 1)
    h = (r // total_mates + lax.rem(r, side) * side) * cores + lax.rem(r // side, cores)
    route = ((g == h) | ((g == 2 * half - 1 - h) & (g >= half))).astype(F32).astype(BF16)
    send1[...] = lax.dot_general(route, pair, NT, preferred_element_type=F32)

    pl.semaphore_wait(barrier, len(mates) + len(rest))

    def block(i):
        return pl.ds(pl.multiple_of(i * side, side), side)

    def remote(src, dst, sems, there):
        return pltpu.make_async_remote_copy(
            src_ref=src, dst_ref=dst, send_sem=sems[0], recv_sem=sems[1], device_id=there, device_id_type=MESH
        )

    own = y * cores + core
    for there in mates:
        remote(send1.at[block(there[0] * cores + there[1])], recv1.at[block(own)], (s1_sem, r1_sem), mate_id(there)).start()
    recv1[block(own)] = send1[block(own)]

    for copy in inputs[2:]:
        copy.wait()

    rows_v = order_v.shape[0]
    lane = iota((1, half), 1)
    device = (lax.rem(lane, total_mates) // cores + lane // total_mates * side) * cores + lax.rem(lane, cores)
    high, low = (order_v[...] // 256).astype(F32).astype(BF16), lax.rem(order_v[...], 256).astype(F32).astype(BF16)
    for p in range(slots):
        place = device * slots + p
        pick = (iota((order_v.shape[1], half), 0) == lax.rem(place, order_v.shape[1])).astype(F32).astype(BF16)
        both = 256.0 * jnp.dot(high, pick, preferred_element_type=F32) + jnp.dot(low, pick, preferred_element_type=F32)
        row = iota((rows_v, half), 0) == place // order_v.shape[1]
        vbuf[p : p + 1] = jnp.sum(jnp.where(row, both, 0.0), 0, keepdims=True)

    most = pl.ds(0, side * (total_mates - 1))
    first_all = remote(send1.at[most], recv1.at[most], (s1_sem, r1_sem), mate_id(mates[0]))
    first_all.wait_recv()
    for i in range(side):
        send2[i] = recv1[pl.ds(i, total_mates, stride=side)].astype(BF16)
    for there in rest:
        remote(send2.at[there[0]], recv2.at[x * side + z], (s2_sem, r2_sem), rest_id(there)).start()
    recv2[x * side + z] = send2[z]

    counts = [nlon_s[w].astype(F32), nlon_s[half - 1 - w].astype(F32)]
    inverse = [1.0 / jnp.full((1, half), n, F32) for n in counts]
    fine = iota((STEP, half), 0).astype(F32)
    for ns in range(2):
        n, inv = counts[ns], inverse[ns]
        for p in range(slots):
            m = vbuf[p : p + 1]
            cb, sb = sincos(m * fine, n, inv, False)
            ca, sa = sincos(m * (STEP * fine), n, inv, False)
            for a in range(SPAN // STEP):
                c1, s1 = ca[a : a + 1], sa[a : a + 1]
                here = pl.ds(a * STEP, STEP)
                table[ns, here, p * half : (p + 1) * half] = (c1 * cb - s1 * sb).astype(BF16)
                table[ns, here, (slots + p) * half : (slots + p + 1) * half] = (-(c1 * sb) - s1 * cb).astype(BF16)

    first = x * quarter
    spans = pl.cdiv(quarter, SPAN)
    starts = (first + SPAN * iota((16, half), 0)).astype(F32)
    for ns in range(2):
        n, inv = counts[ns], inverse[ns]
        for p in range(slots):
            m = vbuf[p : p + 1]
            weight = jnp.where(2.0 * m < n, jnp.where(m == 0.0, 1.0, 2.0), 0.0)
            ct, st = sincos(m * starts, n, inv, True)
            twist[ns, p, 0] = ct * weight
            twist[ns, p, 1] = st * weight

    f16 = iota((STEP, LANES), 0)
    gap = iota((STEP, LANES), 1) - 2 * f16
    parts = [(f16 >= fields * v) & (f16 < fields * (v + 1)) for v in range(levs)]
    picks = []
    for ns in range(2):
        for c in range(2):
            for p in range(slots):
                at = HALF * ns + 2 * fields * p + c
                picks.append(
                    jnp.concatenate(
                        [((gap == at - 2 * fields * v) & parts[v]).astype(F32) for v in range(levs)], 1
                    ).astype(BF16)
                )
    choice = jnp.concatenate(picks, 0)

    most = pl.ds(0, side * levs - 1)
    second_all = remote(recv2.at[most], recv2.at[most], (s2_sem, r2_sem), rest_id(rest[0]))
    second_all.wait_recv()
    arrived = jnp.concatenate(
        [recv2[v * side : (v + 1) * side].reshape(half, LANES) for v in range(levs)], 1
    )
    mixed[...] = lax.dot_general(choice, arrived, NT, preferred_element_type=F32)

    for ns in range(2):
        for p in range(slots):
            at = STEP * (2 * slots * ns + p)
            re, im = mixed[at : at + STEP], mixed[at + STEP * slots : at + STEP * slots + STEP]
            for s in range(spans):
                ct, st = twist[ns, p, 0, s : s + 1], twist[ns, p, 1, s : s + 1]
                here = pl.ds(s * STEP, STEP)
                gbuf[ns, here, p * half : (p + 1) * half] = (re * ct - im * st).astype(BF16)
                gbuf[ns, here, (slots + p) * half : (slots + p + 1) * half] = (re * st + im * ct).astype(BF16)
        grid = lax.dot_general(gbuf[ns], table[ns], NT, preferred_element_type=F32)
        for s in range(spans):
            size = min(SPAN, quarter - s * SPAN)
            place = first + s * SPAN + iota((total, size), 1)
            keep = place < nlon_s[w if ns == 0 else half - 1 - w]
            out_ref[:, ns, s * SPAN : s * SPAN + size] = jnp.where(
                keep, grid[s * STEP : s * STEP + total, :size], 0.0
            )
    first_all.wait_send()
    second_all.wait_send()


def shards(spectral, legendre, wave_order, nlon):
    slots, half, width = legendre.shape
    fields = spectral.shape[1]
    waves, levs = lax.axis_size("wave"), lax.axis_size("lev")
    cores = 2
    chips = waves // cores
    side = math.isqrt(chips)
    quarter = (4 * width + 16) // levs
    spans = pl.cdiv(quarter, SPAN)
    hbm = pl.BlockSpec(memory_space=pltpu.HBM)
    dma = pltpu.SemaphoreType.DMA
    order_rows = wave_order.reshape(-1, min(LANES, wave_order.shape[0] // slots))
    grid = pl.pallas_call(
        functools.partial(kernel, chips, cores, levs, quarter),
        out_shape=pltpu.VMEM((fields * levs, 2, quarter), F32),
        in_specs=[hbm] * 5,
        out_specs=pl.BlockSpec(memory_space=pltpu.VMEM),
        scratch_shapes=[
            pltpu.VMEM(spectral.shape, BF16),
            pltpu.SMEM(wave_order.shape, jnp.int32),
            pltpu.SMEM(nlon.shape, jnp.int32),
            pltpu.VMEM(order_rows.shape, jnp.int32),
            pltpu.VMEM((slots, half, width), BF16),
            pltpu.VMEM((slots, 16, width), F32),
            pltpu.VMEM((LANES, half), F32),
            pltpu.VMEM((half, LANES), F32),
            pltpu.VMEM((half, LANES), F32),
            pltpu.VMEM((side, side * cores, LANES), BF16),
            pltpu.VMEM((levs * side, side * cores, LANES), BF16),
            pltpu.VMEM((2, SPAN, 2 * slots * half), BF16),
            pltpu.VMEM((2, slots, 2, 16, half), F32),
            pltpu.VMEM((4 * slots * STEP, half), F32),
            pltpu.VMEM((2, spans * STEP, 2 * slots * half), BF16),
            pltpu.VMEM((16, half), F32),
            dma((4,)),
            dma((GROUPS,)),
            dma,
            dma,
            dma,
            dma,
        ],
        compiler_params=pltpu.CompilerParams(
            collective_id=0, has_side_effects=True, vmem_limit_bytes=64 * 1024 * 1024 - 400000
        ),
    )(spectral, legendre, wave_order, nlon, order_rows)
    return grid


def solution(mesh):
    placed = (P("wave", "lev", None, None), P("wave", None, None), P(), P())
    return jax.shard_map(
        shards, mesh=mesh, in_specs=placed, out_specs=P(None, "wave", "lev"), check_vma=False
    )
```
